32 devices in a mesh: sec: 2 (over core), lat: 4 (over z), lon: 4 (over y, x).
Axes of the slice: x: 2, y: 2, z: 4, core: 2. Of those that a mesh axis runs over, the one named last changes fastest.
Arguments:
- adjoint: float32 [2, 4, 4, 128, 512], P('sec', None, None, 'lat', 'lon'), may hold values from -6 to 6
- diffusivity: float32 [2, 4, 128, 512], P('sec', None, 'lat', 'lon'), may hold values from 0.02 to 0.2
- velocity: float32 [2, 2, 4, 128, 512], P('sec', None, None, 'lat', 'lon'), may hold values from -0.4 to 0.4
- sensitivity: float32 [2, 4, 4], P('sec'), may hold values from -3 to 3
- sea_mask: int32 [2, 128, 512], P('sec', 'lat', 'lon'), may hold values 0 or 1
- coast_distance: int32 [2, 128, 512], P('sec', 'lat', 'lon'), may hold values from 0 to 31
- send_cells: int32 [2, 4, 12, 1024], P('sec', 'lat', 'lon'), may hold values from 0 to 4095
- recv_slots: int32 [2, 4, 128, 512], P('sec', None, 'lat', 'lon'), may hold values from 0 to 3071
- regrid_weight: float32 [2, 4, 128, 512], P('sec', None, 'lat', 'lon'), may hold values from 0.1 to 0.5
Outputs:
- adjoint_out: float32 [2, 4, 4, 128, 512], P('sec', None, None, 'lat', 'lon')
The draws below stay inside these ranges and needn't reach their ends.
Inputs may be any that keep to these rules, and one draw needn't show every extreme that they name: `send_cells`: a cell number of the sending tile. `recv_slots`: an entry of the 3072 received entries, source tile major, west source first.
All inputs are finite; a program needn't handle non-finite values. No bound on the sum of `sea_mask` on one device may be relied on, other than what follows from the above.
Results may differ from the reference program's by a relative error of at most 0.0003.
Values sent between devices are 32-bit elements; how exact they have to be, the bound alone decides.
A program may use at most 64 MiB of HBM per device.

```python
import math
import jax
import jax.numpy as jnp

TLAT = 32
TLON = 128
LEV = 4
CAP = 1024
COMP = 4
TERMS = 4
STEPS = 2
NLAT = 128
NLON = 512
N_LAT = 4
N_LON = 4


def set_ends(entries, rng, low, top_value):
    longest = entries.shape.index(max(entries.shape))
    spots = []
    for shift in (0, 1):
        where = [jax.random.randint(jax.random.fold_in(rng, axis), (), 0, length) for axis, length in enumerate(entries.shape)]
        where[longest] = (where[longest] + shift) % entries.shape[longest]
        spots.append(tuple(where))
    return entries.at[spots[0]].set(low).at[spots[1]].set(top_value)


def shard_levels(rng, dims, cuts, low, high):
    def one(axis_at, parts):
        draws = jax.random.uniform(jax.random.fold_in(jax.random.fold_in(rng, 6), axis_at), (parts,), jnp.float32, low / len(cuts), high / len(cuts))
        return jnp.repeat(jnp.exp(draws), dims[axis_at] // parts).reshape((-1,) + (1,) * (len(dims) - axis_at - 1))

    factor_of = one(*cuts[0])
    for cut in cuts[1:]:
        factor_of = factor_of * one(*cut)
    return factor_of


def centred(rng, extent, width, most, split=(), kind=jnp.bfloat16):
    result = jax.random.normal(rng, extent, jnp.float32) * width
    if len(split) > 0:
        result = shard_levels(rng, extent, split, -0.22, 0.18) * result
    return jnp.clip(result, min=-most, max=most).astype(kind)


def setup_inputs(seed: int = 0) -> dict:
    streams_of = jax.random.split(jax.random.key(seed), 10)
    return {
        "adjoint": centred(streams_of[0], (2, COMP, LEV, NLAT, NLON), 1.0, 6.0, ((0, 2), (3, 4), (4, 4)), jnp.float32),
        "diffusivity": jnp.clip(jnp.exp(math.log(0.2) - 2.3025851 * jax.random.uniform(streams_of[1], (2, LEV, NLAT, NLON), jnp.float32) ** shard_levels(streams_of[1], (2, LEV, NLAT, NLON), ((0, 2), (2, 4), (3, 4)), -0.2, 0.2)), 0.02, 0.2),
        "velocity": jnp.clip(jax.random.uniform(streams_of[2], (2, 2, LEV, NLAT, NLON), jnp.float32, -0.4, 0.4) * shard_levels(streams_of[2], (2, 2, LEV, NLAT, NLON), ((0, 2), (3, 4), (4, 4)), -0.4, 0.0), -0.4, 0.4),
        "sensitivity": centred(streams_of[3], (2, COMP, COMP), 0.5, 3.0, ((0, 2),), jnp.float32),
        "sea_mask": set_ends((jax.random.randint(streams_of[4], (2, NLAT, NLON), 0, 4) < 3).astype(jnp.int32), jax.random.fold_in(streams_of[4], 1), 0, 1),
        "coast_distance": set_ends(jax.random.randint(streams_of[5], (2, NLAT, NLON), 0, 32), jax.random.fold_in(streams_of[5], 1), 0, 31).astype(jnp.int32),
        "send_cells": set_ends(jax.random.randint(streams_of[6], (2, N_LAT, N_LON * 3, CAP), 0, TLAT * TLON), jax.random.fold_in(streams_of[6], 1), 0, (TLAT * TLON) - 1).astype(jnp.int32),
        "recv_slots": set_ends(jax.random.randint(streams_of[7], (2, TERMS, NLAT, NLON), 0, 3 * CAP), jax.random.fold_in(streams_of[7], 1), 0, (3 * CAP) - 1).astype(jnp.int32),
        "regrid_weight": jnp.clip(0.1 + 0.4 * jax.random.uniform(streams_of[8], (2, TERMS, NLAT, NLON), jnp.float32) ** shard_levels(streams_of[8], (2, TERMS, NLAT, NLON), ((0, 2), (2, 4), (3, 4)), -0.2, 0.2), 0.1, 0.5),
    }


def to_tiles(array):
    lead = array.shape[1]
    shaped = array.reshape(2, lead, N_LAT, TLAT, N_LON, TLON)
    return shaped.transpose(0, 2, 4, 1, 3, 5).reshape(2, N_LAT, N_LON, lead, TLAT * TLON)


def from_tiles(array):
    lead = array.shape[3]
    shaped = array.reshape(2, N_LAT, N_LON, lead, TLAT, TLON)
    return shaped.transpose(0, 3, 1, 4, 2, 5).reshape(2, lead, NLAT, NLON)


def pad_rims(array):
    wrapped = jnp.concatenate([array[..., -1:], array, array[..., :1]], axis=-1)
    widths = [(0, 0)] * (array.ndim - 2) + [(1, 1), (0, 0)]
    return jnp.pad(wrapped, widths)


def sweep_once(field, coef_padded):
    padded = pad_rims(field)
    diffused = coef_padded[:, 0:1] * padded
    carried_x = coef_padded[:, 1:2] * padded
    carried_y = coef_padded[:, 2:3] * padded
    centre = diffused[..., 1:-1, 1:-1]
    laplace = diffused[..., 2:, 1:-1] + diffused[..., :-2, 1:-1] + diffused[..., 1:-1, 2:] + diffused[..., 1:-1, :-2] - 4.0 * centre
    advect = 0.5 * (carried_x[..., 1:-1, 2:] - carried_x[..., 1:-1, :-2]) + 0.5 * (carried_y[..., 2:, 1:-1] - carried_y[..., :-2, 1:-1])
    return field + laplace + advect


def couple(field, sensitivity, weight_sea, send_cells, slot_tiles, weight_tiles):
    surface = field[:, :, 0]
    fluxes = []
    for which in range(COMP):
        total = jnp.zeros((2, NLAT, NLON), jnp.float32)
        for other in range(COMP):
            total = total + sensitivity[:, which, other][:, None, None] * surface[:, other]
        fluxes.append(weight_sea * total)
    flux = jnp.stack(fluxes, axis=1)
    flux_tiles = to_tiles(flux)
    index = send_cells.reshape(2, N_LAT, N_LON, 1, 3 * CAP).astype(jnp.int32)
    index = jnp.broadcast_to(index, (2, N_LAT, N_LON, COMP, 3 * CAP))
    packed = jnp.take_along_axis(flux_tiles, index, axis=4)
    packed = packed.reshape(2, N_LAT, N_LON, COMP, 3, CAP)
    other_side = packed[::-1]
    pieces = []
    for source in range(3):
        rolled = jnp.roll(other_side[:, :, :, :, 2 - source], -(source - 1), axis=2)
        pieces.append(rolled)
    received = jnp.concatenate(pieces, axis=4)
    total = jnp.zeros((2, N_LAT, N_LON, COMP, TLAT * TLON), jnp.float32)
    for which in range(TERMS):
        slots = jnp.broadcast_to(slot_tiles[:, :, :, which:which + 1], (2, N_LAT, N_LON, COMP, TLAT * TLON)).astype(jnp.int32)
        picked = jnp.take_along_axis(received, slots, axis=4)
        total = total + weight_tiles[:, :, :, which:which + 1] * picked
    return from_tiles(total)


def reference(adjoint, diffusivity, velocity, sensitivity, sea_mask, coast_distance, send_cells, recv_slots, regrid_weight):
    distance = coast_distance.astype(jnp.float32)
    blend = (distance + 1.0) / (distance + 9.0)
    weight_sea = sea_mask.astype(jnp.float32) * blend
    coefficients = jnp.concatenate([diffusivity[:, None], velocity], axis=1)
    coef_padded = pad_rims(coefficients)
    slot_tiles = to_tiles(recv_slots)
    weight_tiles = to_tiles(regrid_weight)
    field = adjoint
    for step_index in range(STEPS):
        coupled = couple(field, sensitivity, weight_sea, send_cells, slot_tiles, weight_tiles)
        field = sweep_once(field, coef_padded)
        field = field.at[:, :, 0].add(coupled)
    return field
```

```python
import functools

import jax
import jax.numpy as jnp
from jax import lax
from jax.experimental import pallas as pl
from jax.experimental.pallas import tpu as pltpu
from jax.sharding import PartitionSpec as P

MESH = pl.DeviceIdType.MESH
STEPS = 2
ROWS = 8
LANES = 128
ALONG_LANES = lax.GatherDimensionNumbers(
    offset_dims=(),
    collapsed_slice_dims=(1,),
    start_index_map=(1,),
    operand_batching_dims=(0,),
    start_indices_batching_dims=(0,),
)


def pick_lanes(row, lanes):
    return lax.gather(
        jnp.broadcast_to(row, lanes.shape),
        lanes[..., None],
        ALONG_LANES,
        slice_sizes=(1, 1),
        mode=lax.GatherScatterMode.PROMISE_IN_BOUNDS,
    )


def kernel(
    n_lat,
    n_lon,
    adjoint,
    diffusivity,
    velocity,
    sensitivity,
    sea_mask,
    coast_distance,
    send_cells,
    recv_slots,
    regrid_weight,
    out,
    field,
    coef,
    sea,
    flux,
    cells,
    lists,
    received,
    cols_out,
    cols_east,
    cols_west,
    rows_first,
    rows_last,
    rows_north,
    rows_south,
    list_send,
    list_recv,
    halo_send,
    halo_recv,
):
    comp, lev, tlat, tlon = adjoint.shape
    terms = recv_slots.shape[0]
    blocks = send_cells.shape[1] // LANES
    planes = [(k, l) for k in range(comp) for l in range(lev)]
    sec, lat, lon = (lax.axis_index(name) for name in ("sec", "lat", "lon"))
    other = 1 - sec
    east, west = lax.rem(lon + 1, n_lon), lax.rem(lon + n_lon - 1, n_lon)
    has_south, has_north = lat > 0, lat < n_lat - 1
    sources = (west, lon, east)

    barrier = pltpu.get_barrier_semaphore()

    def greet(sec_to, lat_to, lon_to):
        pl.semaphore_signal(
            barrier, inc=1, device_id=(sec_to, lat_to, lon_to), device_id_type=MESH
        )

    for target in sources:
        greet(other, lat, target)
    greet(sec, lat, west)
    greet(sec, lat, east)
    pl.when(has_south)(lambda: greet(sec, lat - 1, lon))
    pl.when(has_north)(lambda: greet(sec, lat + 1, lon))

    def remote(src, dst, send, recv, device):
        return pltpu.make_async_remote_copy(
            src_ref=src,
            dst_ref=dst,
            send_sem=send,
            recv_sem=recv,
            device_id=device,
            device_id_type=MESH,
        )

    def list_copy(step, d):
        return remote(
            lists.at[step, d],
            received.at[step, 2 - d],
            list_send.at[step, d],
            list_recv.at[step, 2 - d],
            (other, lat, sources[d]),
        )

    def halo_copies(step):
        def one(which, src, dst, device):
            return remote(
                src.at[step],
                dst.at[step],
                halo_send.at[step, which],
                halo_recv.at[step, which],
                device,
            )

        return (
            one(0, cols_out, cols_east, (sec, lat, west)),
            one(1, cols_out, cols_west, (sec, lat, east)),
            one(2, rows_first, rows_north, (sec, lat - 1, lon)),
            one(3, rows_last, rows_south, (sec, lat + 1, lon)),
        )

    lane = lax.broadcasted_iota(jnp.int32, (tlat, tlon), 1)
    line = lax.broadcasted_iota(jnp.int32, (tlat, tlon), 0)

    distance = coast_distance[...].astype(jnp.float32)
    sea[...] = sea_mask[...].astype(jnp.float32) * ((distance + 1.0) / (distance + 9.0))
    for d in range(3):
        for j in range(blocks):
            cells[d, j : j + 1, :] = send_cells[d : d + 1, j * LANES : (j + 1) * LANES]
    for l in range(lev):
        spread = diffusivity[l]
        half_x, half_y = 0.5 * velocity[0, l], 0.5 * velocity[1, l]
        coef[0, l] = spread + half_x
        coef[1, l] = spread - half_x
        coef[2, l] = spread + half_y
        coef[3, l] = spread - half_y
        coef[4, l] = 1.0 - 4.0 * spread

    def send_lists(step, src):
        for k in range(comp):
            total = sensitivity[k, 0] * src[0, 0]
            for j in range(1, comp):
                total = total + sensitivity[k, j] * src[j, 0]
            flux[k] = sea[...] * total
        for d in (0, 2, 1):
            index = cells[d]
            lanes, row = index & (LANES - 1), index >> 7
            found = [jnp.zeros((blocks, LANES), jnp.float32)] * comp
            for r in range(tlat):
                here = row == r
                for k in range(comp):
                    found[k] = jnp.where(
                        here, pick_lanes(flux[k, r : r + 1, :], lanes), found[k]
                    )
            for k in range(comp):
                lists[step, d, k] = found[k]
            if step == 0 and d == 0:
                pl.semaphore_wait(
                    barrier, 5 + has_south.astype(jnp.int32) + has_north.astype(jnp.int32)
                )
            list_copy(step, d).start()

    def inner(step, src, dst):
        packed = jnp.zeros((tlat, tlon), jnp.float32)
        for p, (k, l) in enumerate(planes):
            value = src[k, l]
            to_west = pltpu.roll(coef[0, l] * value, tlon - 1, 1)
            to_east = pltpu.roll(coef[1, l] * value, 1, 1)
            rim = jnp.where(lane == tlon - 1, to_west, to_east)
            packed = jnp.where(lane >> 1 == p, pltpu.roll(rim, 2 * p + 1, 1), packed)
            to_south, to_north = coef[2, l] * value, coef[3, l] * value
            rows_first[step, p : p + 1, :] = to_south[0:1]
            rows_last[step, p : p + 1, :] = to_north[tlat - 1 : tlat]
            dst[k, l] = (
                coef[4, l] * value
                + jnp.where(lane == tlon - 1, 0.0, to_west)
                + jnp.where(lane == 0, 0.0, to_east)
                + jnp.where(line == tlat - 1, 0.0, pltpu.roll(to_south, tlat - 1, 0))
                + jnp.where(line == 0, 0.0, pltpu.roll(to_north, 1, 0))
            )
        cols_out[step] = packed
        copies = halo_copies(step)
        copies[0].start()
        copies[1].start()
        pl.when(has_south)(copies[2].start)
        pl.when(has_north)(copies[3].start)

    def rims(step, dst):
        copies = halo_copies(step)
        copies[0].wait_recv()
        copies[1].wait_recv()
        both = jnp.where(lane & 1 == 0, cols_east[step], cols_west[step])
        edge = (lane == 0) | (lane == tlon - 1)
        for p, (k, l) in enumerate(planes):
            turned = pltpu.roll(both, tlon - 1 - 2 * p, 1)
            dst[k, l] = dst[k, l] + jnp.where(edge, turned, 0.0)

        @pl.when(has_north)
        def _():
            copies[2].wait_recv()
            for p, (k, l) in enumerate(planes):
                dst[k, l, tlat - 1 : tlat, :] += rows_north[step, p : p + 1, :]

        @pl.when(has_south)
        def _():
            copies[3].wait_recv()
            for p, (k, l) in enumerate(planes):
                dst[k, l, 0:1, :] += rows_south[step, p : p + 1, :]

    def regrid(step, dst):
        for d in range(3):
            list_copy(step, d).wait_recv()

        def some(g, carry):
            where = pl.ds(pl.multiple_of(g * ROWS, ROWS), ROWS)
            index = [recv_slots[t, where, :] for t in range(terms)]
            lanes = [i & (LANES - 1) for i in index]
            row = [i >> 7 for i in index]
            found = [[jnp.zeros((ROWS, tlon), jnp.float32)] * comp for t in range(terms)]
            for r in range(3 * blocks):
                here = [i == r for i in row]
                for k in range(comp):
                    source = received[step, r // blocks, k, r % blocks : r % blocks + 1, :]
                    for t in range(terms):
                        found[t][k] = jnp.where(
                            here[t], pick_lanes(source, lanes[t]), found[t][k]
                        )
            for k in range(comp):
                total = dst[k, 0, where, :]
                for t in range(terms):
                    total = total + regrid_weight[t, where, :] * found[t][k]
                dst[k, 0, where, :] = total
            return carry

        lax.fori_loop(0, tlat // ROWS, some, 0)

    for step, (src, dst) in enumerate(((adjoint, field), (field, out))):
        send_lists(step, src)
        inner(step, src, dst)
        rims(step, dst)
        regrid(step, dst)

    for step in range(STEPS):
        for d in range(3):
            list_copy(step, d).wait_send()
        copies = halo_copies(step)
        copies[0].wait_send()
        copies[1].wait_send()
        pl.when(has_south)(copies[2].wait_send)
        pl.when(has_north)(copies[3].wait_send)


def on_device(n_lat, n_lon, *arrays):
    arrays = [array[0] for array in arrays]
    arrays[6] = arrays[6][0]
    adjoint, send_cells = arrays[0], arrays[6]
    comp, lev, tlat, tlon = adjoint.shape
    blocks = send_cells.shape[1] // LANES
    planes = comp * lev
    vmem = pl.BlockSpec(memory_space=pltpu.VMEM)
    specs = [vmem] * len(arrays)
    specs[3] = pl.BlockSpec(memory_space=pltpu.SMEM)
    f32 = jnp.float32
    result = pl.pallas_call(
        functools.partial(kernel, n_lat, n_lon),
        out_shape=jax.ShapeDtypeStruct(adjoint.shape, f32),
        in_specs=specs,
        out_specs=vmem,
        scratch_shapes=[
            pltpu.VMEM(adjoint.shape, f32),
            pltpu.VMEM((5, lev, tlat, tlon), f32),
            pltpu.VMEM((tlat, tlon), f32),
            pltpu.VMEM((comp, tlat, tlon), f32),
            pltpu.VMEM((3, blocks, LANES), jnp.int32),
            pltpu.VMEM((STEPS, 3, comp, blocks, LANES), f32),
            pltpu.VMEM((STEPS, 3, comp, blocks, LANES), f32),
            pltpu.VMEM((STEPS, tlat, tlon), f32),
            pltpu.VMEM((STEPS, tlat, tlon), f32),
            pltpu.VMEM((STEPS, tlat, tlon), f32),
            pltpu.VMEM((STEPS, planes, tlon), f32),
            pltpu.VMEM((STEPS, planes, tlon), f32),
            pltpu.VMEM((STEPS, planes, tlon), f32),
            pltpu.VMEM((STEPS, planes, tlon), f32),
            pltpu.SemaphoreType.DMA((STEPS, 3)),
            pltpu.SemaphoreType.DMA((STEPS, 3)),
            pltpu.SemaphoreType.DMA((STEPS, 4)),
            pltpu.SemaphoreType.DMA((STEPS, 4)),
        ],
        compiler_params=pltpu.CompilerParams(
            collective_id=0, has_side_effects=True, vmem_limit_bytes=16 * 1024 * 1024
        ),
        cost_estimate=pl.CostEstimate(
            flops=4_000_000, bytes_accessed=900_000, transcendentals=0
        ),
    )(*arrays)
    return result[None]


def solution(mesh):
    placed = (
        P("sec", None, None, "lat", "lon"),
        P("sec", None, "lat", "lon"),
        P("sec", None, None, "lat", "lon"),
        P("sec", None, None),
        P("sec", "lat", "lon"),
        P("sec", "lat", "lon"),
        P("sec", "lat", "lon", None),
        P("sec", None, "lat", "lon"),
        P("sec", None, "lat", "lon"),
    )
    return jax.shard_map(
        functools.partial(on_device, mesh.shape["lat"], mesh.shape["lon"]),
        mesh=mesh,
        in_specs=placed,
        out_specs=P("sec", None, None, "lat", "lon"),
        check_vma=False,
    )
```

```python
import functools

import jax
import jax.numpy as jnp
from jax import lax
from jax.experimental import pallas as pl
from jax.experimental.pallas import tpu as pltpu
from jax.sharding import PartitionSpec as P

MESH = pl.DeviceIdType.MESH
STEPS = 2
ROWS = 8
LANES = 128
ALONG_LANES = lax.GatherDimensionNumbers(
    offset_dims=(),
    collapsed_slice_dims=(1,),
    start_index_map=(1,),
    operand_batching_dims=(0,),
    start_indices_batching_dims=(0,),
)


def pick_lanes(row, lanes):
    return lax.gather(
        jnp.broadcast_to(row, lanes.shape),
        lanes[..., None],
        ALONG_LANES,
        slice_sizes=(1, 1),
        mode=lax.GatherScatterMode.PROMISE_IN_BOUNDS,
    )


def kernel(
    n_lat,
    n_lon,
    *refs,
):
    inputs, out = refs[:9], refs[9]
    held, (
    field,
    coef,
    sea,
    flux,
    lists,
    received,
    cols_out,
    cols_east,
    cols_west,
    rows_first,
    rows_last,
    rows_north,
    rows_south,
    list_send,
    list_recv,
    halo_send,
    halo_recv,
    load_sem,
    ) = refs[10:19], refs[19:]
    (
        adjoint,
        diffusivity,
        velocity,
        sensitivity,
        sea_mask,
        coast_distance,
        cells,
        recv_slots,
        regrid_weight,
    ) = held
    loads = [
        pltpu.make_async_copy(inputs[i], held[i], load_sem.at[i]) for i in range(9)
    ]
    for i in (0, 6, 4, 5, 3, 1, 2, 7, 8):
        loads[i].start()

    comp, lev, tlat, tlon = adjoint.shape
    terms = recv_slots.shape[0]
    blocks = cells.shape[1]
    planes = [(k, l) for k in range(comp) for l in range(lev)]
    sec, lat, lon = (lax.axis_index(name) for name in ("sec", "lat", "lon"))
    other = 1 - sec
    east, west = lax.rem(lon + 1, n_lon), lax.rem(lon + n_lon - 1, n_lon)
    has_south, has_north = lat > 0, lat < n_lat - 1
    sources = (west, lon, east)

    barrier = pltpu.get_barrier_semaphore()

    def greet(sec_to, lat_to, lon_to):
        pl.semaphore_signal(
            barrier, inc=1, device_id=(sec_to, lat_to, lon_to), device_id_type=MESH
        )

    for target in sources:
        greet(other, lat, target)
    greet(sec, lat, west)
    greet(sec, lat, east)
    pl.when(has_south)(lambda: greet(sec, lat - 1, lon))
    pl.when(has_north)(lambda: greet(sec, lat + 1, lon))

    def remote(src, dst, send, recv, device):
        return pltpu.make_async_remote_copy(
            src_ref=src,
            dst_ref=dst,
            send_sem=send,
            recv_sem=recv,
            device_id=device,
            device_id_type=MESH,
        )

    def list_copy(step, d):
        return remote(
            lists.at[step, d],
            received.at[step, 2 - d],
            list_send.at[step, d],
            list_recv.at[step, 2 - d],
            (other, lat, sources[d]),
        )

    def halo_copies(step):
        def one(which, src, dst, device):
            return remote(
                src.at[step],
                dst.at[step],
                halo_send.at[step, which],
                halo_recv.at[step, which],
                device,
            )

        return (
            one(0, cols_out, cols_east, (sec, lat, west)),
            one(1, cols_out, cols_west, (sec, lat, east)),
            one(2, rows_first, rows_north, (sec, lat - 1, lon)),
            one(3, rows_last, rows_south, (sec, lat + 1, lon)),
        )

    lane = lax.broadcasted_iota(jnp.int32, (tlat, tlon), 1)
    line = lax.broadcasted_iota(jnp.int32, (tlat, tlon), 0)

    for i in (4, 5, 3, 0, 6):
        loads[i].wait()
    distance = coast_distance[...].astype(jnp.float32)
    sea[...] = sea_mask[...].astype(jnp.float32) * ((distance + 1.0) / (distance + 9.0))

    def coefficients():
        loads[1].wait()
        loads[2].wait()
        for l in range(lev):
            spread = diffusivity[l]
            half_x, half_y = 0.5 * velocity[0, l], 0.5 * velocity[1, l]
            coef[0, l] = spread + half_x
            coef[1, l] = spread - half_x
            coef[2, l] = spread + half_y
            coef[3, l] = spread - half_y
            coef[4, l] = 1.0 - 4.0 * spread

    def send_lists(step, src):
        for k in range(comp):
            total = sensitivity[k, 0] * src[0, 0]
            for j in range(1, comp):
                total = total + sensitivity[k, j] * src[j, 0]
            flux[k] = sea[...] * total
        for d in (0, 2, 1):
            index = cells[d]
            lanes, row = index & (LANES - 1), index >> 7
            found = [jnp.zeros((blocks, LANES), jnp.float32)] * comp
            for r in range(tlat):
                here = row == r
                for k in range(comp):
                    found[k] = jnp.where(
                        here, pick_lanes(flux[k, r : r + 1, :], lanes), found[k]
                    )
            for k in range(comp):
                lists[step, d, k] = found[k]
            if step == 0 and d == 0:
                pl.semaphore_wait(
                    barrier, 5 + has_south.astype(jnp.int32) + has_north.astype(jnp.int32)
                )
            list_copy(step, d).start()

    def inner(step, src, dst):
        packed = jnp.zeros((tlat, tlon), jnp.float32)
        for p, (k, l) in enumerate(planes):
            value = src[k, l]
            to_west = pltpu.roll(coef[0, l] * value, tlon - 1, 1)
            to_east = pltpu.roll(coef[1, l] * value, 1, 1)
            rim = jnp.where(lane == tlon - 1, to_west, to_east)
            packed = jnp.where(lane >> 1 == p, pltpu.roll(rim, 2 * p + 1, 1), packed)
            to_south, to_north = coef[2, l] * value, coef[3, l] * value
            rows_first[step, p : p + 1, :] = to_south[0:1]
            rows_last[step, p : p + 1, :] = to_north[tlat - 1 : tlat]
            dst[k, l] = (
                coef[4, l] * value
                + jnp.where(lane == tlon - 1, 0.0, to_west)
                + jnp.where(lane == 0, 0.0, to_east)
                + jnp.where(line == tlat - 1, 0.0, pltpu.roll(to_south, tlat - 1, 0))
                + jnp.where(line == 0, 0.0, pltpu.roll(to_north, 1, 0))
            )
        cols_out[step] = packed
        copies = halo_copies(step)
        copies[0].start()
        copies[1].start()
        pl.when(has_south)(copies[2].start)
        pl.when(has_north)(copies[3].start)

    def rims(step, dst):
        copies = halo_copies(step)
        copies[0].wait_recv()
        copies[1].wait_recv()
        both = jnp.where(lane & 1 == 0, cols_east[step], cols_west[step])
        edge = (lane == 0) | (lane == tlon - 1)
        for p, (k, l) in enumerate(planes):
            turned = pltpu.roll(both, tlon - 1 - 2 * p, 1)
            dst[k, l] = dst[k, l] + jnp.where(edge, turned, 0.0)

        @pl.when(has_north)
        def _():
            copies[2].wait_recv()
            for p, (k, l) in enumerate(planes):
                dst[k, l, tlat - 1 : tlat, :] += rows_north[step, p : p + 1, :]

        @pl.when(has_south)
        def _():
            copies[3].wait_recv()
            for p, (k, l) in enumerate(planes):
                dst[k, l, 0:1, :] += rows_south[step, p : p + 1, :]

    def regrid(step, dst):
        for d in range(3):
            list_copy(step, d).wait_recv()

        def some(g, carry):
            where = pl.ds(pl.multiple_of(g * ROWS, ROWS), ROWS)
            index = [recv_slots[t, where, :] for t in range(terms)]
            lanes = [i & (LANES - 1) for i in index]
            row = [i >> 7 for i in index]
            found = [[jnp.zeros((ROWS, tlon), jnp.float32)] * comp for t in range(terms)]
            for t in range(terms):
                for r in range(3 * blocks):
                    here = row[t] == r
                    for k in range(comp):
                        source = received[step, r // blocks, k, r % blocks : r % blocks + 1, :]
                        found[t][k] = jnp.where(here, pick_lanes(source, lanes[t]), found[t][k])
            for k in range(comp):
                total = dst[k, 0, where, :]
                for t in range(terms):
                    total = total + regrid_weight[t, where, :] * found[t][k]
                dst[k, 0, where, :] = total
            return carry

        lax.fori_loop(0, tlat // ROWS, some, 0)

    for step, (src, dst) in enumerate(((adjoint, field), (field, out))):
        send_lists(step, src)
        if step == 0:
            coefficients()
        inner(step, src, dst)
        rims(step, dst)
        if step == 0:
            loads[7].wait()
            loads[8].wait()
        regrid(step, dst)

    for step in range(STEPS):
        for d in range(3):
            list_copy(step, d).wait_send()
        copies = halo_copies(step)
        copies[0].wait_send()
        copies[1].wait_send()
        pl.when(has_south)(copies[2].wait_send)
        pl.when(has_north)(copies[3].wait_send)


def on_device(n_lat, n_lon, *arrays):
    arrays = [array[0] for array in arrays]
    blocks = arrays[6].shape[2] // LANES
    arrays[6] = arrays[6].reshape(3, blocks, LANES)
    adjoint = arrays[0]
    comp, lev, tlat, tlon = adjoint.shape
    planes = comp * lev
    vmem = pl.BlockSpec(memory_space=pltpu.VMEM)
    specs = [pl.BlockSpec(memory_space=pltpu.HBM)] * len(arrays)
    spaces = [pltpu.SMEM if i == 3 else pltpu.VMEM for i in range(len(arrays))]
    f32 = jnp.float32
    result = pl.pallas_call(
        functools.partial(kernel, n_lat, n_lon),
        out_shape=jax.ShapeDtypeStruct(adjoint.shape, f32),
        in_specs=specs,
        out_specs=vmem,
        scratch_shapes=[
            *(space(array.shape, array.dtype) for space, array in zip(spaces, arrays)),
            pltpu.VMEM(adjoint.shape, f32),
            pltpu.VMEM((5, lev, tlat, tlon), f32),
            pltpu.VMEM((tlat, tlon), f32),
            pltpu.VMEM((comp, tlat, tlon), f32),
            pltpu.VMEM((STEPS, 3, comp, blocks, LANES), f32),
            pltpu.VMEM((STEPS, 3, comp, blocks, LANES), f32),
            pltpu.VMEM((STEPS, tlat, tlon), f32),
            pltpu.VMEM((STEPS, tlat, tlon), f32),
            pltpu.VMEM((STEPS, tlat, tlon), f32),
            pltpu.VMEM((STEPS, planes, tlon), f32),
            pltpu.VMEM((STEPS, planes, tlon), f32),
            pltpu.VMEM((STEPS, planes, tlon), f32),
            pltpu.VMEM((STEPS, planes, tlon), f32),
            pltpu.SemaphoreType.DMA((STEPS, 3)),
            pltpu.SemaphoreType.DMA((STEPS, 3)),
            pltpu.SemaphoreType.DMA((STEPS, 4)),
            pltpu.SemaphoreType.DMA((STEPS, 4)),
            pltpu.SemaphoreType.DMA((len(arrays),)),
        ],
        compiler_params=pltpu.CompilerParams(
            collective_id=0, has_side_effects=True, vmem_limit_bytes=60 * 1024 * 1024
        ),
        cost_estimate=pl.CostEstimate(
            flops=4_000_000, bytes_accessed=900_000, transcendentals=0
        ),
    )(*arrays)
    return result[None]


def solution(mesh):
    placed = (
        P("sec", None, None, "lat", "lon"),
        P("sec", None, "lat", "lon"),
        P("sec", None, None, "lat", "lon"),
        P("sec", None, None),
        P("sec", "lat", "lon"),
        P("sec", "lat", "lon"),
        P("sec", "lat", "lon", None),
        P("sec", None, "lat", "lon"),
        P("sec", None, "lat", "lon"),
    )
    return jax.shard_map(
        functools.partial(on_device, mesh.shape["lat"], mesh.shape["lon"]),
        mesh=mesh,
        in_specs=placed,
        out_specs=P("sec", None, None, "lat", "lon"),
        check_vma=False,
    )
```

```python
import functools

import jax
import jax.numpy as jnp
from jax import lax
from jax.experimental import pallas as pl
from jax.experimental.pallas import tpu as pltpu
from jax.sharding import PartitionSpec as P

MESH = pl.DeviceIdType.MESH
STEPS = 2
ROWS = 8
LANES = 128
ALONG_LANES = lax.GatherDimensionNumbers(
    offset_dims=(),
    collapsed_slice_dims=(1,),
    start_index_map=(1,),
    operand_batching_dims=(0,),
    start_indices_batching_dims=(0,),
)


def pick_lanes(row, lanes):
    return lax.gather(
        jnp.broadcast_to(row, lanes.shape),
        lanes[..., None],
        ALONG_LANES,
        slice_sizes=(1, 1),
        mode=lax.GatherScatterMode.PROMISE_IN_BOUNDS,
    )


def kernel(
    n_lat,
    n_lon,
    *refs,
):
    inputs, out = refs[:9], refs[9]
    held, (
    field,
    coef,
    sea,
    flux,
    lists,
    received,
    cols_out,
    cols_east,
    cols_west,
    rows_first,
    rows_last,
    rows_north,
    rows_south,
    list_send,
    list_recv,
    halo_send,
    halo_recv,
    load_sem,
    ) = refs[10:19], refs[19:]
    (
        adjoint,
        diffusivity,
        velocity,
        sensitivity,
        sea_mask,
        coast_distance,
        cells,
        recv_slots,
        regrid_weight,
    ) = held
    loads = [
        pltpu.make_async_copy(inputs[i], held[i], load_sem.at[i]) for i in range(9)
    ]
    for i in (0, 6, 4, 5, 3, 1, 2, 7, 8):
        loads[i].start()

    comp, lev, tlat, tlon = adjoint.shape
    terms = recv_slots.shape[0]
    blocks = cells.shape[1]
    planes = [(k, l) for k in range(comp) for l in range(lev)]
    sec, lat, lon = (lax.axis_index(name) for name in ("sec", "lat", "lon"))
    other = 1 - sec
    east, west = lax.rem(lon + 1, n_lon), lax.rem(lon + n_lon - 1, n_lon)
    has_south, has_north = lat > 0, lat < n_lat - 1
    sources = (west, lon, east)

    barrier = pltpu.get_barrier_semaphore()

    def greet(sec_to, lat_to, lon_to):
        pl.semaphore_signal(
            barrier, inc=1, device_id=(sec_to, lat_to, lon_to), device_id_type=MESH
        )

    for target in sources:
        greet(other, lat, target)
    greet(sec, lat, west)
    greet(sec, lat, east)
    pl.when(has_south)(lambda: greet(sec, lat - 1, lon))
    pl.when(has_north)(lambda: greet(sec, lat + 1, lon))

    def remote(src, dst, send, recv, device):
        return pltpu.make_async_remote_copy(
            src_ref=src,
            dst_ref=dst,
            send_sem=send,
            recv_sem=recv,
            device_id=device,
            device_id_type=MESH,
        )

    def list_copy(step, d):
        return remote(
            lists.at[step, d],
            received.at[step, 2 - d],
            list_send.at[step, d],
            list_recv.at[step, 2 - d],
            (other, lat, sources[d]),
        )

    def halo_copies(step):
        def one(which, src, dst, device):
            return remote(
                src.at[step],
                dst.at[step],
                halo_send.at[step, which],
                halo_recv.at[step, which],
                device,
            )

        return (
            one(0, cols_out, cols_east, (sec, lat, west)),
            one(1, cols_out, cols_west, (sec, lat, east)),
            one(2, rows_first, rows_north, (sec, lat - 1, lon)),
            one(3, rows_last, rows_south, (sec, lat + 1, lon)),
        )

    lane = lax.broadcasted_iota(jnp.int32, (tlat, tlon), 1)
    line = lax.broadcasted_iota(jnp.int32, (tlat, tlon), 0)

    for i in (4, 5, 3, 0, 6):
        loads[i].wait()
    distance = coast_distance[...].astype(jnp.float32)
    sea[...] = sea_mask[...].astype(jnp.float32) * ((distance + 1.0) / (distance + 9.0))

    def coefficients():
        loads[1].wait()
        loads[2].wait()
        for l in range(lev):
            spread = diffusivity[l]
            half_x, half_y = 0.5 * velocity[0, l], 0.5 * velocity[1, l]
            coef[0, l] = spread + half_x
            coef[1, l] = spread - half_x
            coef[2, l] = spread + half_y
            coef[3, l] = spread - half_y
            coef[4, l] = 1.0 - 4.0 * spread

    def send_lists(step, src):
        for k in range(comp):
            total = sensitivity[k, 0] * src[0, 0]
            for j in range(1, comp):
                total = total + sensitivity[k, j] * src[j, 0]
            flux[k] = sea[...] * total
        for d in (0, 2, 1):
            index = cells[d]
            lanes, row = index & (LANES - 1), index >> 7
            found = [jnp.zeros((blocks, LANES), jnp.float32)] * comp
            for r in range(tlat):
                here = row == r
                for k in range(comp):
                    found[k] = jnp.where(
                        here, pick_lanes(flux[k, r : r + 1, :], lanes), found[k]
                    )
            for k in range(comp):
                lists[step, d, k] = found[k]
            if step == 0 and d == 0:
                pl.semaphore_wait(
                    barrier, 5 + has_south.astype(jnp.int32) + has_north.astype(jnp.int32)
                )
            list_copy(step, d).start()

    def inner(step, src, dst):
        packed = jnp.zeros((tlat, tlon), jnp.float32)
        for p, (k, l) in enumerate(planes):
            value = src[k, l]
            to_west = pltpu.roll(coef[0, l] * value, tlon - 1, 1)
            to_east = pltpu.roll(coef[1, l] * value, 1, 1)
            rim = jnp.where(lane == tlon - 1, to_west, to_east)
            packed = jnp.where(lane >> 1 == p, pltpu.roll(rim, 2 * p + 1, 1), packed)
            to_south, to_north = coef[2, l] * value, coef[3, l] * value
            rows_first[step, p : p + 1, :] = to_south[0:1]
            rows_last[step, p : p + 1, :] = to_north[tlat - 1 : tlat]
            dst[k, l] = (
                coef[4, l] * value
                + jnp.where(lane == tlon - 1, 0.0, to_west)
                + jnp.where(lane == 0, 0.0, to_east)
                + jnp.where(line == tlat - 1, 0.0, pltpu.roll(to_south, tlat - 1, 0))
                + jnp.where(line == 0, 0.0, pltpu.roll(to_north, 1, 0))
            )
        cols_out[step] = packed
        copies = halo_copies(step)
        copies[0].start()
        copies[1].start()
        pl.when(has_south)(copies[2].start)
        pl.when(has_north)(copies[3].start)

    def rims(step, dst):
        copies = halo_copies(step)
        copies[0].wait_recv()
        copies[1].wait_recv()
        both = jnp.where(lane & 1 == 0, cols_east[step], cols_west[step])
        edge = (lane == 0) | (lane == tlon - 1)
        for p, (k, l) in enumerate(planes):
            turned = pltpu.roll(both, tlon - 1 - 2 * p, 1)
            dst[k, l] = dst[k, l] + jnp.where(edge, turned, 0.0)

        @pl.when(has_north)
        def _():
            copies[2].wait_recv()
            for p, (k, l) in enumerate(planes):
                dst[k, l, tlat - 1 : tlat, :] += rows_north[step, p : p + 1, :]

        @pl.when(has_south)
        def _():
            copies[3].wait_recv()
            for p, (k, l) in enumerate(planes):
                dst[k, l, 0:1, :] += rows_south[step, p : p + 1, :]

    def regrid(step, dst):
        for d in range(3):
            list_copy(step, d).wait_recv()

        def some(g, carry):
            where = pl.ds(pl.multiple_of(g * ROWS, ROWS), ROWS)
            index = [recv_slots[t, where, :] for t in range(terms)]
            lanes = [i & (LANES - 1) for i in index]
            row = [i >> 7 for i in index]
            found = [[jnp.zeros((ROWS, tlon), jnp.float32)] * comp for t in range(terms)]
            for t in range(terms):
                for r in range(3 * blocks):
                    here = row[t] == r
                    for k in range(comp):
                        source = received[step, r // blocks, k, r % blocks : r % blocks + 1, :]
                        found[t][k] = jnp.where(here, pick_lanes(source, lanes[t]), found[t][k])
            for k in range(comp):
                total = dst[k, 0, where, :]
                for t in range(terms):
                    total = total + regrid_weight[t, where, :] * found[t][k]
                dst[k, 0, where, :] = total
            return carry

        lax.fori_loop(0, tlat // ROWS, some, 0, unroll=True)

    for step, (src, dst) in enumerate(((adjoint, field), (field, out))):
        send_lists(step, src)
        if step == 0:
            coefficients()
        inner(step, src, dst)
        rims(step, dst)
        if step == 0:
            loads[7].wait()
            loads[8].wait()
        regrid(step, dst)

    for step in range(STEPS):
        for d in range(3):
            list_copy(step, d).wait_send()
        copies = halo_copies(step)
        copies[0].wait_send()
        copies[1].wait_send()
        pl.when(has_south)(copies[2].wait_send)
        pl.when(has_north)(copies[3].wait_send)


def on_device(n_lat, n_lon, *arrays):
    arrays = [array[0] for array in arrays]
    blocks = arrays[6].shape[2] // LANES
    arrays[6] = arrays[6].reshape(3, blocks, LANES)
    adjoint = arrays[0]
    comp, lev, tlat, tlon = adjoint.shape
    planes = comp * lev
    vmem = pl.BlockSpec(memory_space=pltpu.VMEM)
    specs = [pl.BlockSpec(memory_space=pltpu.HBM)] * len(arrays)
    spaces = [pltpu.SMEM if i == 3 else pltpu.VMEM for i in range(len(arrays))]
    f32 = jnp.float32
    arrays = [pltpu.with_memory_space_constraint(a, pltpu.HBM) for a in arrays]
    result = pl.pallas_call(
        functools.partial(kernel, n_lat, n_lon),
        out_shape=jax.ShapeDtypeStruct(adjoint.shape, f32),
        in_specs=specs,
        out_specs=vmem,
        scratch_shapes=[
            *(space(array.shape, array.dtype) for space, array in zip(spaces, arrays)),
            pltpu.VMEM(adjoint.shape, f32),
            pltpu.VMEM((5, lev, tlat, tlon), f32),
            pltpu.VMEM((tlat, tlon), f32),
            pltpu.VMEM((comp, tlat, tlon), f32),
            pltpu.VMEM((STEPS, 3, comp, blocks, LANES), f32),
            pltpu.VMEM((STEPS, 3, comp, blocks, LANES), f32),
            pltpu.VMEM((STEPS, tlat, tlon), f32),
            pltpu.VMEM((STEPS, tlat, tlon), f32),
            pltpu.VMEM((STEPS, tlat, tlon), f32),
            pltpu.VMEM((STEPS, planes, tlon), f32),
            pltpu.VMEM((STEPS, planes, tlon), f32),
            pltpu.VMEM((STEPS, planes, tlon), f32),
            pltpu.VMEM((STEPS, planes, tlon), f32),
            pltpu.SemaphoreType.DMA((STEPS, 3)),
            pltpu.SemaphoreType.DMA((STEPS, 3)),
            pltpu.SemaphoreType.DMA((STEPS, 4)),
            pltpu.SemaphoreType.DMA((STEPS, 4)),
            pltpu.SemaphoreType.DMA((len(arrays),)),
        ],
        compiler_params=pltpu.CompilerParams(
            collective_id=0, has_side_effects=True, vmem_limit_bytes=16 * 1024 * 1024
        ),
        cost_estimate=pl.CostEstimate(
            flops=4_000_000, bytes_accessed=900_000, transcendentals=0
        ),
    )(*arrays)
    return result[None]


def solution(mesh):
    placed = (
        P("sec", None, None, "lat", "lon"),
        P("sec", None, "lat", "lon"),
        P("sec", None, None, "lat", "lon"),
        P("sec", None, None),
        P("sec", "lat", "lon"),
        P("sec", "lat", "lon"),
        P("sec", "lat", "lon", None),
        P("sec", None, "lat", "lon"),
        P("sec", None, "lat", "lon"),
    )
    return jax.shard_map(
        functools.partial(on_device, mesh.shape["lat"], mesh.shape["lon"]),
        mesh=mesh,
        in_specs=placed,
        out_specs=P("sec", None, None, "lat", "lon"),
        check_vma=False,
    )
```

```python
import functools

import jax
import jax.numpy as jnp
from jax import lax
from jax.experimental import pallas as pl
from jax.experimental.pallas import tpu as pltpu
from jax.sharding import PartitionSpec as P

MESH = pl.DeviceIdType.MESH
STEPS = 2
ROWS = 8
LANES = 128
ALONG_LANES = lax.GatherDimensionNumbers(
    offset_dims=(),
    collapsed_slice_dims=(1,),
    start_index_map=(1,),
    operand_batching_dims=(0,),
    start_indices_batching_dims=(0,),
)


def pick_lanes(row, lanes):
    return lax.gather(
        jnp.broadcast_to(row, lanes.shape),
        lanes[..., None],
        ALONG_LANES,
        slice_sizes=(1, 1),
        mode=lax.GatherScatterMode.PROMISE_IN_BOUNDS,
    )


def kernel(
    n_lat,
    n_lon,
    *refs,
):
    inputs, out = refs[:9], refs[9]
    held, (
    field,
    coef,
    sea,
    flux,
    wide,
    lists,
    received,
    cols_out,
    cols_east,
    cols_west,
    rows_first,
    rows_last,
    rows_north,
    rows_south,
    list_send,
    list_recv,
    halo_send,
    halo_recv,
    load_sem,
    ) = refs[10:19], refs[19:]
    (
        adjoint,
        diffusivity,
        velocity,
        sensitivity,
        sea_mask,
        coast_distance,
        cells,
        recv_slots,
        regrid_weight,
    ) = held
    loads = [
        pltpu.make_async_copy(inputs[i], held[i], load_sem.at[i]) for i in range(9)
    ]
    for i in (0, 6, 4, 5, 3, 1, 2, 7, 8):
        loads[i].start()

    comp, lev, tlat, tlon = adjoint.shape
    terms = recv_slots.shape[0]
    blocks = cells.shape[1]
    planes = [(k, l) for k in range(comp) for l in range(lev)]
    sec, lat, lon = (lax.axis_index(name) for name in ("sec", "lat", "lon"))
    other = 1 - sec
    east, west = lax.rem(lon + 1, n_lon), lax.rem(lon + n_lon - 1, n_lon)
    has_south, has_north = lat > 0, lat < n_lat - 1
    sources = (west, lon, east)

    barrier = pltpu.get_barrier_semaphore()

    def greet(sec_to, lat_to, lon_to):
        pl.semaphore_signal(
            barrier, inc=1, device_id=(sec_to, lat_to, lon_to), device_id_type=MESH
        )

    for target in sources:
        greet(other, lat, target)
    greet(sec, lat, west)
    greet(sec, lat, east)
    pl.when(has_south)(lambda: greet(sec, lat - 1, lon))
    pl.when(has_north)(lambda: greet(sec, lat + 1, lon))

    def remote(src, dst, send, recv, device):
        return pltpu.make_async_remote_copy(
            src_ref=src,
            dst_ref=dst,
            send_sem=send,
            recv_sem=recv,
            device_id=device,
            device_id_type=MESH,
        )

    def list_copy(step, d):
        return remote(
            lists.at[step, d],
            received.at[step, 2 - d],
            list_send.at[step, d],
            list_recv.at[step, 2 - d],
            (other, lat, sources[d]),
        )

    def halo_copies(step):
        def one(which, src, dst, device):
            return remote(
                src.at[step],
                dst.at[step],
                halo_send.at[step, which],
                halo_recv.at[step, which],
                device,
            )

        return (
            one(0, cols_out, cols_east, (sec, lat, west)),
            one(1, cols_out, cols_west, (sec, lat, east)),
            one(2, rows_first, rows_north, (sec, lat - 1, lon)),
            one(3, rows_last, rows_south, (sec, lat + 1, lon)),
        )

    lane = lax.broadcasted_iota(jnp.int32, (tlat, tlon), 1)
    line = lax.broadcasted_iota(jnp.int32, (tlat, tlon), 0)

    for i in (4, 5, 3, 0, 6):
        loads[i].wait()
    distance = coast_distance[...].astype(jnp.float32)
    sea[...] = sea_mask[...].astype(jnp.float32) * ((distance + 1.0) / (distance + 9.0))

    def coefficients():
        loads[1].wait()
        loads[2].wait()
        for l in range(lev):
            spread = diffusivity[l]
            half_x, half_y = 0.5 * velocity[0, l], 0.5 * velocity[1, l]
            coef[0, l] = spread + half_x
            coef[1, l] = spread - half_x
            coef[2, l] = spread + half_y
            coef[3, l] = spread - half_y
            coef[4, l] = 1.0 - 4.0 * spread

    def send_lists(step, src):
        for k in range(comp):
            total = sensitivity[k, 0] * src[0, 0]
            for j in range(1, comp):
                total = total + sensitivity[k, j] * src[j, 0]
            flux[k] = sea[...] * total
        for d in (0, 2, 1):
            index = cells[d]
            lanes, row = index & (LANES - 1), index >> 7
            found = [jnp.zeros((blocks, LANES), jnp.float32)] * comp
            for r in range(tlat):
                here = row == r
                for k in range(comp):
                    found[k] = jnp.where(
                        here, pick_lanes(flux[k, r : r + 1, :], lanes), found[k]
                    )
            for k in range(comp):
                lists[step, d, k] = found[k]
            if step == 0 and d == 0:
                pl.semaphore_wait(
                    barrier, 5 + has_south.astype(jnp.int32) + has_north.astype(jnp.int32)
                )
            list_copy(step, d).start()

    def inner(step, src, dst):
        packed = jnp.zeros((tlat, tlon), jnp.float32)
        for p, (k, l) in enumerate(planes):
            value = src[k, l]
            to_west = pltpu.roll(coef[0, l] * value, tlon - 1, 1)
            to_east = pltpu.roll(coef[1, l] * value, 1, 1)
            rim = jnp.where(lane == tlon - 1, to_west, to_east)
            packed = jnp.where(lane >> 1 == p, pltpu.roll(rim, 2 * p + 1, 1), packed)
            to_south, to_north = coef[2, l] * value, coef[3, l] * value
            rows_first[step, p : p + 1, :] = to_south[0:1]
            rows_last[step, p : p + 1, :] = to_north[tlat - 1 : tlat]
            dst[k, l] = (
                coef[4, l] * value
                + jnp.where(lane == tlon - 1, 0.0, to_west)
                + jnp.where(lane == 0, 0.0, to_east)
                + jnp.where(line == tlat - 1, 0.0, pltpu.roll(to_south, tlat - 1, 0))
                + jnp.where(line == 0, 0.0, pltpu.roll(to_north, 1, 0))
            )
        cols_out[step] = packed
        copies = halo_copies(step)
        copies[0].start()
        copies[1].start()
        pl.when(has_south)(copies[2].start)
        pl.when(has_north)(copies[3].start)

    def rims(step, dst):
        copies = halo_copies(step)
        copies[0].wait_recv()
        copies[1].wait_recv()
        both = jnp.where(lane & 1 == 0, cols_east[step], cols_west[step])
        edge = (lane == 0) | (lane == tlon - 1)
        for p, (k, l) in enumerate(planes):
            turned = pltpu.roll(both, tlon - 1 - 2 * p, 1)
            dst[k, l] = dst[k, l] + jnp.where(edge, turned, 0.0)

        @pl.when(has_north)
        def _():
            copies[2].wait_recv()
            for p, (k, l) in enumerate(planes):
                dst[k, l, tlat - 1 : tlat, :] += rows_north[step, p : p + 1, :]

        @pl.when(has_south)
        def _():
            copies[3].wait_recv()
            for p, (k, l) in enumerate(planes):
                dst[k, l, 0:1, :] += rows_south[step, p : p + 1, :]

    def regrid(step, dst, e):
        list_copy(step, 2 - e).wait_recv()
        for k in range(comp):
            for j in range(blocks):
                wide[k, j] = jnp.broadcast_to(
                    received[step, e, k, j : j + 1, :], (ROWS, LANES)
                )
        for g in range(tlat // ROWS):
            where = slice(g * ROWS, (g + 1) * ROWS)
            total = [dst[k, 0, where, :] for k in range(comp)]
            for t in range(terms):
                index = recv_slots[t, where, :]
                weight = regrid_weight[t, where, :]
                lanes, row = index & (LANES - 1), index >> 7
                found = [jnp.zeros((ROWS, tlon), jnp.float32)] * comp
                for j in range(blocks):
                    here = row == e * blocks + j
                    for k in range(comp):
                        found[k] = jnp.where(here, pick_lanes(wide[k, j], lanes), found[k])
                for k in range(comp):
                    total[k] = total[k] + weight * found[k]
            for k in range(comp):
                dst[k, 0, where, :] = total[k]

    for step, (src, dst) in enumerate(((adjoint, field), (field, out))):
        send_lists(step, src)
        if step == 0:
            coefficients()
        inner(step, src, dst)
        if step == 0:
            loads[7].wait()
            loads[8].wait()
        regrid(step, dst, 1)
        rims(step, dst)
        regrid(step, dst, 0)
        regrid(step, dst, 2)

    for step in range(STEPS):
        for d in range(3):
            list_copy(step, d).wait_send()
        copies = halo_copies(step)
        copies[0].wait_send()
        copies[1].wait_send()
        pl.when(has_south)(copies[2].wait_send)
        pl.when(has_north)(copies[3].wait_send)


def on_device(n_lat, n_lon, *arrays):
    arrays = [array[0] for array in arrays]
    blocks = arrays[6].shape[2] // LANES
    arrays[6] = arrays[6].reshape(3, blocks, LANES)
    adjoint = arrays[0]
    comp, lev, tlat, tlon = adjoint.shape
    planes = comp * lev
    vmem = pl.BlockSpec(memory_space=pltpu.VMEM)
    specs = [pl.BlockSpec(memory_space=pltpu.HBM)] * len(arrays)
    spaces = [pltpu.SMEM if i == 3 else pltpu.VMEM for i in range(len(arrays))]
    f32 = jnp.float32
    arrays = [pltpu.with_memory_space_constraint(a, pltpu.HBM) for a in arrays]
    result = pl.pallas_call(
        functools.partial(kernel, n_lat, n_lon),
        out_shape=jax.ShapeDtypeStruct(adjoint.shape, f32),
        in_specs=specs,
        out_specs=vmem,
        scratch_shapes=[
            *(space(array.shape, array.dtype) for space, array in zip(spaces, arrays)),
            pltpu.VMEM(adjoint.shape, f32),
            pltpu.VMEM((5, lev, tlat, tlon), f32),
            pltpu.VMEM((tlat, tlon), f32),
            pltpu.VMEM((comp, tlat, tlon), f32),
            pltpu.VMEM((comp, blocks, ROWS, LANES), f32),
            pltpu.VMEM((STEPS, 3, comp, blocks, LANES), f32),
            pltpu.VMEM((STEPS, 3, comp, blocks, LANES), f32),
            pltpu.VMEM((STEPS, tlat, tlon), f32),
            pltpu.VMEM((STEPS, tlat, tlon), f32),
            pltpu.VMEM((STEPS, tlat, tlon), f32),
            pltpu.VMEM((STEPS, planes, tlon), f32),
            pltpu.VMEM((STEPS, planes, tlon), f32),
            pltpu.VMEM((STEPS, planes, tlon), f32),
            pltpu.VMEM((STEPS, planes, tlon), f32),
            pltpu.SemaphoreType.DMA((STEPS, 3)),
            pltpu.SemaphoreType.DMA((STEPS, 3)),
            pltpu.SemaphoreType.DMA((STEPS, 4)),
            pltpu.SemaphoreType.DMA((STEPS, 4)),
            pltpu.SemaphoreType.DMA((len(arrays),)),
        ],
        compiler_params=pltpu.CompilerParams(
            collective_id=0, has_side_effects=True, vmem_limit_bytes=16 * 1024 * 1024
        ),
        cost_estimate=pl.CostEstimate(
            flops=4_000_000, bytes_accessed=900_000, transcendentals=0
        ),
    )(*arrays)
    return result[None]


def solution(mesh):
    placed = (
        P("sec", None, None, "lat", "lon"),
        P("sec", None, "lat", "lon"),
        P("sec", None, None, "lat", "lon"),
        P("sec", None, None),
        P("sec", "lat", "lon"),
        P("sec", "lat", "lon"),
        P("sec", "lat", "lon", None),
        P("sec", None, "lat", "lon"),
        P("sec", None, "lat", "lon"),
    )
    return jax.shard_map(
        functools.partial(on_device, mesh.shape["lat"], mesh.shape["lon"]),
        mesh=mesh,
        in_specs=placed,
        out_specs=P("sec", None, None, "lat", "lon"),
        check_vma=False,
    )
```

```python
import functools

import jax
import jax.numpy as jnp
from jax import lax
from jax.experimental import pallas as pl
from jax.experimental.pallas import tpu as pltpu
from jax.sharding import PartitionSpec as P

MESH = pl.DeviceIdType.MESH
STEPS = 2
ROWS = 8
LANES = 128
ALONG_LANES = lax.GatherDimensionNumbers(
    offset_dims=(),
    collapsed_slice_dims=(1,),
    start_index_map=(1,),
    operand_batching_dims=(0,),
    start_indices_batching_dims=(0,),
)


def pick_lanes(row, lanes):
    return lax.gather(
        jnp.broadcast_to(row, lanes.shape),
        lanes[..., None],
        ALONG_LANES,
        slice_sizes=(1, 1),
        mode=lax.GatherScatterMode.PROMISE_IN_BOUNDS,
    )


def kernel(
    n_lat,
    n_lon,
    *refs,
):
    inputs, out = refs[:9], refs[9]
    held, (
    field,
    coef,
    sea,
    flux,
    wide,
    lists,
    received,
    cols_out,
    cols_east,
    cols_west,
    rows_first,
    rows_last,
    rows_north,
    rows_south,
    list_send,
    list_recv,
    halo_send,
    halo_recv,
    load_sem,
    ) = refs[10:19], refs[19:]
    (
        adjoint,
        diffusivity,
        velocity,
        sensitivity,
        sea_mask,
        coast_distance,
        cells,
        recv_slots,
        regrid_weight,
    ) = held
    loads = [
        pltpu.make_async_copy(inputs[i], held[i], load_sem.at[i]) for i in range(9)
    ]
    for i in (0, 6, 4, 5, 3, 1, 2, 7, 8):
        loads[i].start()

    comp, lev, tlat, tlon = adjoint.shape
    terms = recv_slots.shape[0]
    blocks = cells.shape[1]
    planes = [(k, l) for k in range(comp) for l in range(lev)]
    sec, lat, lon = (lax.axis_index(name) for name in ("sec", "lat", "lon"))
    other = 1 - sec
    east, west = lax.rem(lon + 1, n_lon), lax.rem(lon + n_lon - 1, n_lon)
    has_south, has_north = lat > 0, lat < n_lat - 1
    sources = (west, lon, east)

    barrier = pltpu.get_barrier_semaphore()

    def greet(sec_to, lat_to, lon_to):
        pl.semaphore_signal(
            barrier, inc=1, device_id=(sec_to, lat_to, lon_to), device_id_type=MESH
        )

    for target in sources:
        greet(other, lat, target)
    greet(sec, lat, west)
    greet(sec, lat, east)
    pl.when(has_south)(lambda: greet(sec, lat - 1, lon))
    pl.when(has_north)(lambda: greet(sec, lat + 1, lon))

    def remote(src, dst, send, recv, device):
        return pltpu.make_async_remote_copy(
            src_ref=src,
            dst_ref=dst,
            send_sem=send,
            recv_sem=recv,
            device_id=device,
            device_id_type=MESH,
        )

    def list_copy(step, d):
        return remote(
            lists.at[step, d],
            received.at[step, 2 - d],
            list_send.at[step, d],
            list_recv.at[step, 2 - d],
            (other, lat, sources[d]),
        )

    def halo_copies(step):
        def one(which, src, dst, device):
            return remote(
                src.at[step],
                dst.at[step],
                halo_send.at[step, which],
                halo_recv.at[step, which],
                device,
            )

        return (
            one(0, cols_out, cols_east, (sec, lat, west)),
            one(1, cols_out, cols_west, (sec, lat, east)),
            one(2, rows_first, rows_north, (sec, lat - 1, lon)),
            one(3, rows_last, rows_south, (sec, lat + 1, lon)),
        )

    lane = lax.broadcasted_iota(jnp.int32, (tlat, tlon), 1)
    line = lax.broadcasted_iota(jnp.int32, (tlat, tlon), 0)

    for i in (4, 5, 3, 0, 6):
        loads[i].wait()
    distance = coast_distance[...].astype(jnp.float32)
    sea[...] = sea_mask[...].astype(jnp.float32) * ((distance + 1.0) / (distance + 9.0))

    def coefficients():
        loads[1].wait()
        loads[2].wait()
        for l in range(lev):
            spread = diffusivity[l]
            half_x, half_y = 0.5 * velocity[0, l], 0.5 * velocity[1, l]
            coef[0, l] = spread + half_x
            coef[1, l] = spread - half_x
            coef[2, l] = spread + half_y
            coef[3, l] = spread - half_y
            coef[4, l] = 1.0 - 4.0 * spread

    def send_lists(step, src):
        for k in range(comp):
            total = sensitivity[k, 0] * src[0, 0]
            for j in range(1, comp):
                total = total + sensitivity[k, j] * src[j, 0]
            flux[k] = sea[...] * total
        for d in (0, 2, 1):
            index = cells[d]
            lanes, row = index & (LANES - 1), index >> 7
            found = [jnp.zeros((blocks, LANES), jnp.float32)] * comp
            for r in range(tlat):
                here = row == r
                for k in range(comp):
                    found[k] = jnp.where(
                        here, pick_lanes(flux[k, r : r + 1, :], lanes), found[k]
                    )
            for k in range(comp):
                lists[step, d, k] = found[k]
            if step == 0 and d == 0:
                pl.semaphore_wait(
                    barrier, 5 + has_south.astype(jnp.int32) + has_north.astype(jnp.int32)
                )
            list_copy(step, d).start()

    def inner(step, src, dst):
        packed = jnp.zeros((tlat, tlon), jnp.float32)
        for p, (k, l) in enumerate(planes):
            value = src[k, l]
            to_west = pltpu.roll(coef[0, l] * value, tlon - 1, 1)
            to_east = pltpu.roll(coef[1, l] * value, 1, 1)
            rim = jnp.where(lane == tlon - 1, to_west, to_east)
            packed = jnp.where(lane >> 1 == p, pltpu.roll(rim, 2 * p + 1, 1), packed)
            to_south, to_north = coef[2, l] * value, coef[3, l] * value
            rows_first[step, p : p + 1, :] = to_south[0:1]
            rows_last[step, p : p + 1, :] = to_north[tlat - 1 : tlat]
            dst[k, l] = (
                coef[4, l] * value
                + jnp.where(lane == tlon - 1, 0.0, to_west)
                + jnp.where(lane == 0, 0.0, to_east)
                + jnp.where(line == tlat - 1, 0.0, pltpu.roll(to_south, tlat - 1, 0))
                + jnp.where(line == 0, 0.0, pltpu.roll(to_north, 1, 0))
            )
        cols_out[step] = packed
        copies = halo_copies(step)
        copies[0].start()
        copies[1].start()
        pl.when(has_south)(copies[2].start)
        pl.when(has_north)(copies[3].start)

    def rims(step, dst, levels, arrive):
        copies = halo_copies(step)
        if arrive:
            copies[0].wait_recv()
            copies[1].wait_recv()
        both = jnp.where(lane & 1 == 0, cols_east[step], cols_west[step])
        edge = (lane == 0) | (lane == tlon - 1)
        chosen = [(p, k, l) for p, (k, l) in enumerate(planes) if l in levels]
        for p, k, l in chosen:
            turned = pltpu.roll(both, tlon - 1 - 2 * p, 1)
            dst[k, l] = dst[k, l] + jnp.where(edge, turned, 0.0)

        @pl.when(has_north)
        def _():
            if arrive:
                copies[2].wait_recv()
            for p, k, l in chosen:
                dst[k, l, tlat - 1 : tlat, :] += rows_north[step, p : p + 1, :]

        @pl.when(has_south)
        def _():
            if arrive:
                copies[3].wait_recv()
            for p, k, l in chosen:
                dst[k, l, 0:1, :] += rows_south[step, p : p + 1, :]

    def regrid(step, dst, e):
        list_copy(step, 2 - e).wait_recv()
        for k in range(comp):
            for j in range(blocks):
                wide[k, j] = jnp.broadcast_to(
                    received[step, e, k, j : j + 1, :], (ROWS, LANES)
                )
        for g in range(tlat // ROWS):
            where = slice(g * ROWS, (g + 1) * ROWS)
            total = [dst[k, 0, where, :] for k in range(comp)]
            for t in range(terms):
                index = recv_slots[t, where, :]
                weight = regrid_weight[t, where, :]
                lanes, row = index & (LANES - 1), index >> 7
                found = [jnp.zeros((ROWS, tlon), jnp.float32)] * comp
                for j in range(blocks):
                    here = row == e * blocks + j
                    for k in range(comp):
                        found[k] = jnp.where(here, pick_lanes(wide[k, j], lanes), found[k])
                for k in range(comp):
                    total[k] = total[k] + weight * found[k]
            for k in range(comp):
                dst[k, 0, where, :] = total[k]

    deep = range(1, lev)
    for step, (src, dst) in enumerate(((adjoint, field), (field, out))):
        send_lists(step, src)
        if step == 0:
            coefficients()
        else:
            rims(step - 1, src, deep, False)
        inner(step, src, dst)
        if step == 0:
            loads[7].wait()
            loads[8].wait()
        regrid(step, dst, 1)
        regrid(step, dst, 2)
        if step == STEPS - 1:
            rims(step, dst, range(lev), True)
        regrid(step, dst, 0)
        if step < STEPS - 1:
            rims(step, dst, (0,), True)

    for step in range(STEPS):
        for d in range(3):
            list_copy(step, d).wait_send()
        copies = halo_copies(step)
        copies[0].wait_send()
        copies[1].wait_send()
        pl.when(has_south)(copies[2].wait_send)
        pl.when(has_north)(copies[3].wait_send)


def on_device(n_lat, n_lon, *arrays):
    arrays = [array[0] for array in arrays]
    blocks = arrays[6].shape[2] // LANES
    arrays[6] = arrays[6].reshape(3, blocks, LANES)
    adjoint = arrays[0]
    comp, lev, tlat, tlon = adjoint.shape
    planes = comp * lev
    vmem = pl.BlockSpec(memory_space=pltpu.VMEM)
    specs = [pl.BlockSpec(memory_space=pltpu.HBM)] * len(arrays)
    spaces = [pltpu.SMEM if i == 3 else pltpu.VMEM for i in range(len(arrays))]
    f32 = jnp.float32
    arrays = [pltpu.with_memory_space_constraint(a, pltpu.HBM) for a in arrays]
    result = pl.pallas_call(
        functools.partial(kernel, n_lat, n_lon),
        out_shape=jax.ShapeDtypeStruct(adjoint.shape, f32),
        in_specs=specs,
        out_specs=vmem,
        scratch_shapes=[
            *(space(array.shape, array.dtype) for space, array in zip(spaces, arrays)),
            pltpu.VMEM(adjoint.shape, f32),
            pltpu.VMEM((5, lev, tlat, tlon), f32),
            pltpu.VMEM((tlat, tlon), f32),
            pltpu.VMEM((comp, tlat, tlon), f32),
            pltpu.VMEM((comp, blocks, ROWS, LANES), f32),
            pltpu.VMEM((STEPS, 3, comp, blocks, LANES), f32),
            pltpu.VMEM((STEPS, 3, comp, blocks, LANES), f32),
            pltpu.VMEM((STEPS, tlat, tlon), f32),
            pltpu.VMEM((STEPS, tlat, tlon), f32),
            pltpu.VMEM((STEPS, tlat, tlon), f32),
            pltpu.VMEM((STEPS, planes, tlon), f32),
            pltpu.VMEM((STEPS, planes, tlon), f32),
            pltpu.VMEM((STEPS, planes, tlon), f32),
            pltpu.VMEM((STEPS, planes, tlon), f32),
            pltpu.SemaphoreType.DMA((STEPS, 3)),
            pltpu.SemaphoreType.DMA((STEPS, 3)),
            pltpu.SemaphoreType.DMA((STEPS, 4)),
            pltpu.SemaphoreType.DMA((STEPS, 4)),
            pltpu.SemaphoreType.DMA((len(arrays),)),
        ],
        compiler_params=pltpu.CompilerParams(
            collective_id=0, has_side_effects=True, vmem_limit_bytes=16 * 1024 * 1024
        ),
        cost_estimate=pl.CostEstimate(
            flops=4_000_000, bytes_accessed=900_000, transcendentals=0
        ),
    )(*arrays)
    return result[None]


def solution(mesh):
    placed = (
        P("sec", None, None, "lat", "lon"),
        P("sec", None, "lat", "lon"),
        P("sec", None, None, "lat", "lon"),
        P("sec", None, None),
        P("sec", "lat", "lon"),
        P("sec", "lat", "lon"),
        P("sec", "lat", "lon", None),
        P("sec", None, "lat", "lon"),
        P("sec", None, "lat", "lon"),
    )
    return jax.shard_map(
        functools.partial(on_device, mesh.shape["lat"], mesh.shape["lon"]),
        mesh=mesh,
        in_specs=placed,
        out_specs=P("sec", None, None, "lat", "lon"),
        check_vma=False,
    )
```

```python
import functools

import jax
import jax.numpy as jnp
from jax import lax
from jax.experimental import pallas as pl
from jax.experimental.pallas import tpu as pltpu
from jax.sharding import PartitionSpec as P

MESH = pl.DeviceIdType.MESH
STEPS = 2
ROWS = 8
LANES = 128
ALONG_LANES = lax.GatherDimensionNumbers(
    offset_dims=(),
    collapsed_slice_dims=(1,),
    start_index_map=(1,),
    operand_batching_dims=(0,),
    start_indices_batching_dims=(0,),
)


def pick_lanes(row, lanes):
    return lax.gather(
        jnp.broadcast_to(row, lanes.shape),
        lanes[..., None],
        ALONG_LANES,
        slice_sizes=(1, 1),
        mode=lax.GatherScatterMode.PROMISE_IN_BOUNDS,
    )


def kernel(
    n_lat,
    n_lon,
    *refs,
):
    inputs, out = refs[:9], refs[9]
    held, (
    field,
    coef,
    sea,
    flux,
    wide,
    lists,
    received,
    cols_out,
    cols_east,
    cols_west,
    rows_first,
    rows_last,
    rows_north,
    rows_south,
    list_send,
    list_recv,
    halo_send,
    halo_recv,
    load_sem,
    ) = refs[10:19], refs[19:]
    (
        adjoint,
        diffusivity,
        velocity,
        sensitivity,
        sea_mask,
        coast_distance,
        cells,
        recv_slots,
        regrid_weight,
    ) = held
    loads = [
        pltpu.make_async_copy(inputs[i], held[i], load_sem.at[i]) for i in range(9)
    ]
    for i in (0, 6, 4, 5, 3, 1, 2, 7, 8):
        loads[i].start()

    comp, lev, tlat, tlon = adjoint.shape
    terms = recv_slots.shape[0]
    blocks = cells.shape[1]
    planes = [(k, l) for k in range(comp) for l in range(lev)]
    sec, lat, lon = (lax.axis_index(name) for name in ("sec", "lat", "lon"))
    other = 1 - sec
    east, west = lax.rem(lon + 1, n_lon), lax.rem(lon + n_lon - 1, n_lon)
    has_south, has_north = lat > 0, lat < n_lat - 1
    sources = (west, lon, east)

    barrier = pltpu.get_barrier_semaphore()

    def greet(sec_to, lat_to, lon_to):
        pl.semaphore_signal(
            barrier, inc=1, device_id=(sec_to, lat_to, lon_to), device_id_type=MESH
        )

    for target in sources:
        greet(other, lat, target)
    greet(sec, lat, west)
    greet(sec, lat, east)
    pl.when(has_south)(lambda: greet(sec, lat - 1, lon))
    pl.when(has_north)(lambda: greet(sec, lat + 1, lon))

    def remote(src, dst, send, recv, device):
        return pltpu.make_async_remote_copy(
            src_ref=src,
            dst_ref=dst,
            send_sem=send,
            recv_sem=recv,
            device_id=device,
            device_id_type=MESH,
        )

    def list_copy(step, d):
        return remote(
            lists.at[step, d],
            received.at[step, 2 - d],
            list_send.at[step, d],
            list_recv.at[step, 2 - d],
            (other, lat, sources[d]),
        )

    def halo_copies(step):
        def one(which, src, dst, device):
            return remote(
                src.at[step],
                dst.at[step],
                halo_send.at[step, which],
                halo_recv.at[step, which],
                device,
            )

        return (
            one(0, cols_out, cols_east, (sec, lat, west)),
            one(1, cols_out, cols_west, (sec, lat, east)),
            one(2, rows_first, rows_north, (sec, lat - 1, lon)),
            one(3, rows_last, rows_south, (sec, lat + 1, lon)),
        )

    lane = lax.broadcasted_iota(jnp.int32, (tlat, tlon), 1)
    line = lax.broadcasted_iota(jnp.int32, (tlat, tlon), 0)

    for i in (4, 5, 3, 0, 6):
        loads[i].wait()
    distance = coast_distance[...].astype(jnp.float32)
    sea[...] = sea_mask[...].astype(jnp.float32) * ((distance + 1.0) / (distance + 9.0))

    def coefficients():
        loads[1].wait()
        loads[2].wait()
        for l in range(lev):
            spread = diffusivity[l]
            half_x, half_y = 0.5 * velocity[0, l], 0.5 * velocity[1, l]
            coef[0, l] = spread + half_x
            coef[1, l] = spread - half_x
            coef[2, l] = spread + half_y
            coef[3, l] = spread - half_y
            coef[4, l] = 1.0 - 4.0 * spread
            coef[5, l] = jnp.where(lane == 0, spread + half_x, spread - half_x)

    def send_lists(step, src):
        for k in range(comp):
            total = sensitivity[k, 0] * src[0, 0]
            for j in range(1, comp):
                total = total + sensitivity[k, j] * src[j, 0]
            flux[k] = sea[...] * total
        for d in (0, 2, 1):
            index = cells[d]
            lanes, row = index & (LANES - 1), index >> 7
            found = [jnp.zeros((blocks, LANES), jnp.float32)] * comp
            for r in range(tlat):
                here = row == r
                for k in range(comp):
                    found[k] = jnp.where(
                        here, pick_lanes(flux[k, r : r + 1, :], lanes), found[k]
                    )
            for k in range(comp):
                lists[step, d, k] = found[k]
            if step == 0 and d == 0:
                pl.semaphore_wait(
                    barrier, 5 + has_south.astype(jnp.int32) + has_north.astype(jnp.int32)
                )
            list_copy(step, d).start()

    def send_rims(step, src):
        packed = jnp.zeros((tlat, tlon), jnp.float32)
        for p, (k, l) in enumerate(planes):
            value = src[k, l]
            rim = coef[5, l] * value
            turned = pltpu.roll(rim, (2 * p + 2) % tlon, 1)
            packed = jnp.where((lane + 1) >> 1 == p + 1, turned, packed)
            rows_first[step, p : p + 1, :] = coef[2, l, 0:1, :] * src[k, l, 0:1, :]
            rows_last[step, p : p + 1, :] = (
                coef[3, l, tlat - 1 : tlat, :] * src[k, l, tlat - 1 : tlat, :]
            )
        cols_out[step] = packed
        copies = halo_copies(step)
        copies[0].start()
        copies[1].start()
        pl.when(has_south)(copies[2].start)
        pl.when(has_north)(copies[3].start)

    def inner(src, dst):
        for k, l in planes:
            value = src[k, l]
            to_west = pltpu.roll(coef[0, l] * value, tlon - 1, 1)
            to_east = pltpu.roll(coef[1, l] * value, 1, 1)
            to_south, to_north = coef[2, l] * value, coef[3, l] * value
            dst[k, l] = (
                coef[4, l] * value
                + jnp.where(lane == tlon - 1, 0.0, to_west)
                + jnp.where(lane == 0, 0.0, to_east)
                + jnp.where(line == tlat - 1, 0.0, pltpu.roll(to_south, tlat - 1, 0))
                + jnp.where(line == 0, 0.0, pltpu.roll(to_north, 1, 0))
            )

    def rims(step, dst, levels, arrive):
        copies = halo_copies(step)
        if arrive:
            copies[0].wait_recv()
            copies[1].wait_recv()
        from_east = pltpu.roll(cols_east[step], tlon - 2, 1)
        both = jnp.where(lane & 1 == 0, from_east, cols_west[step])
        edge = (lane == 0) | (lane == tlon - 1)
        chosen = [(p, k, l) for p, (k, l) in enumerate(planes) if l in levels]
        for p, k, l in chosen:
            turned = pltpu.roll(both, tlon - 1 - 2 * p, 1)
            dst[k, l] = dst[k, l] + jnp.where(edge, turned, 0.0)

        @pl.when(has_north)
        def _():
            if arrive:
                copies[2].wait_recv()
            for p, k, l in chosen:
                dst[k, l, tlat - 1 : tlat, :] += rows_north[step, p : p + 1, :]

        @pl.when(has_south)
        def _():
            if arrive:
                copies[3].wait_recv()
            for p, k, l in chosen:
                dst[k, l, 0:1, :] += rows_south[step, p : p + 1, :]

    def regrid(step, dst, e):
        list_copy(step, 2 - e).wait_recv()
        for k in range(comp):
            for j in range(blocks):
                wide[k, j] = jnp.broadcast_to(
                    received[step, e, k, j : j + 1, :], (ROWS, LANES)
                )
        for g in range(tlat // ROWS):
            where = slice(g * ROWS, (g + 1) * ROWS)
            total = [dst[k, 0, where, :] for k in range(comp)]
            for t in range(terms):
                index = recv_slots[t, where, :]
                weight = regrid_weight[t, where, :]
                lanes, row = index & (LANES - 1), index >> 7
                found = [jnp.zeros((ROWS, tlon), jnp.float32)] * comp
                for j in range(blocks):
                    here = row == e * blocks + j
                    for k in range(comp):
                        found[k] = jnp.where(here, pick_lanes(wide[k, j], lanes), found[k])
                for k in range(comp):
                    total[k] = total[k] + weight * found[k]
            for k in range(comp):
                dst[k, 0, where, :] = total[k]

    deep = range(1, lev)
    for step, (src, dst) in enumerate(((adjoint, field), (field, out))):
        send_lists(step, src)
        if step == 0:
            coefficients()
        else:
            rims(step - 1, src, deep, False)
        send_rims(step, src)
        inner(src, dst)
        if step == 0:
            loads[7].wait()
            loads[8].wait()
        regrid(step, dst, 1)
        regrid(step, dst, 2)
        if step == STEPS - 1:
            rims(step, dst, range(lev), True)
        regrid(step, dst, 0)
        if step < STEPS - 1:
            rims(step, dst, (0,), True)

    for step in range(STEPS):
        for d in range(3):
            list_copy(step, d).wait_send()
        copies = halo_copies(step)
        copies[0].wait_send()
        copies[1].wait_send()
        pl.when(has_south)(copies[2].wait_send)
        pl.when(has_north)(copies[3].wait_send)


def on_device(n_lat, n_lon, *arrays):
    arrays = [array[0] for array in arrays]
    blocks = arrays[6].shape[2] // LANES
    arrays[6] = arrays[6].reshape(3, blocks, LANES)
    adjoint = arrays[0]
    comp, lev, tlat, tlon = adjoint.shape
    planes = comp * lev
    vmem = pl.BlockSpec(memory_space=pltpu.VMEM)
    specs = [pl.BlockSpec(memory_space=pltpu.HBM)] * len(arrays)
    spaces = [pltpu.SMEM if i == 3 else pltpu.VMEM for i in range(len(arrays))]
    f32 = jnp.float32
    arrays = [pltpu.with_memory_space_constraint(a, pltpu.HBM) for a in arrays]
    result = pl.pallas_call(
        functools.partial(kernel, n_lat, n_lon),
        out_shape=jax.ShapeDtypeStruct(adjoint.shape, f32),
        in_specs=specs,
        out_specs=vmem,
        scratch_shapes=[
            *(space(array.shape, array.dtype) for space, array in zip(spaces, arrays)),
            pltpu.VMEM(adjoint.shape, f32),
            pltpu.VMEM((6, lev, tlat, tlon), f32),
            pltpu.VMEM((tlat, tlon), f32),
            pltpu.VMEM((comp, tlat, tlon), f32),
            pltpu.VMEM((comp, blocks, ROWS, LANES), f32),
            pltpu.VMEM((STEPS, 3, comp, blocks, LANES), f32),
            pltpu.VMEM((STEPS, 3, comp, blocks, LANES), f32),
            pltpu.VMEM((STEPS, tlat, tlon), f32),
            pltpu.VMEM((STEPS, tlat, tlon), f32),
            pltpu.VMEM((STEPS, tlat, tlon), f32),
            pltpu.VMEM((STEPS, planes, tlon), f32),
            pltpu.VMEM((STEPS, planes, tlon), f32),
            pltpu.VMEM((STEPS, planes, tlon), f32),
            pltpu.VMEM((STEPS, planes, tlon), f32),
            pltpu.SemaphoreType.DMA((STEPS, 3)),
            pltpu.SemaphoreType.DMA((STEPS, 3)),
            pltpu.SemaphoreType.DMA((STEPS, 4)),
            pltpu.SemaphoreType.DMA((STEPS, 4)),
            pltpu.SemaphoreType.DMA((len(arrays),)),
        ],
        compiler_params=pltpu.CompilerParams(
            collective_id=0, has_side_effects=True, vmem_limit_bytes=16 * 1024 * 1024
        ),
        cost_estimate=pl.CostEstimate(
            flops=4_000_000, bytes_accessed=900_000, transcendentals=0
        ),
    )(*arrays)
    return result[None]


def solution(mesh):
    placed = (
        P("sec", None, None, "lat", "lon"),
        P("sec", None, "lat", "lon"),
        P("sec", None, None, "lat", "lon"),
        P("sec", None, None),
        P("sec", "lat", "lon"),
        P("sec", "lat", "lon"),
        P("sec", "lat", "lon", None),
        P("sec", None, "lat", "lon"),
        P("sec", None, "lat", "lon"),
    )
    return jax.shard_map(
        functools.partial(on_device, mesh.shape["lat"], mesh.shape["lon"]),
        mesh=mesh,
        in_specs=placed,
        out_specs=P("sec", None, None, "lat", "lon"),
        check_vma=False,
    )
```
